32 devices in a mesh: groups: 2 (over x), ctx: 16 (over z, y, core).
Axes of the slice: x: 2, y: 2, z: 4, core: 2. Of those that a mesh axis runs over, the one named last changes fastest.
Arguments:
- queries: bfloat16 [4096, 2048], P(('groups', 'ctx')), parts along dimension 0, may hold values from -22 to 22
- key_rows: bfloat16 [4096, 512], P(('groups', 'ctx')), parts along dimension 0, may hold values from -4 to 4
- value_rows: bfloat16 [4096, 512], P(('groups', 'ctx')), parts along dimension 0, may hold values from -6 to 6
- output_gradient: bfloat16 [4096, 2048], P(('groups', 'ctx')), parts along dimension 0, may hold values from -6 to 6
- lengths: int32 [16], P('groups'), parts along dimension 0, may hold values from 1 to 512, 2048 in all
Outputs:
- attended: bfloat16 [4096, 2048], P(('groups', 'ctx')), parts along dimension 0
- grad_queries: bfloat16 [4096, 2048], P(('groups', 'ctx')), parts along dimension 0
- key_gradient: bfloat16 [4096, 512], P(('groups', 'ctx')), parts along dimension 0
- value_gradient: bfloat16 [4096, 512], P(('groups', 'ctx')), parts along dimension 0
The draws below stay inside these ranges and needn't reach their ends.
There are 2 independent parts, one for each index of `groups`. The reference program is written for one: setup_inputs(seed, part) draws one part's arguments, and reference() takes and returns one part's arrays. A program takes and returns all parts, laid end to end along the dimension named above; each array names one. Nothing has to cross between parts.
Inputs may be any that keep to these rules, and one draw needn't show every extreme that they name: `lengths`: each document has 1 to 512 tokens, one exactly 512; they sum to 2048.
All inputs are finite; a program needn't handle non-finite values.
Results may differ from the reference program's by a relative error of at most 0.035.
Values may be sent and summed in bfloat16 or wider, within the bound.
A program may use at most 128 MiB of HBM per device.

```python
import math
import jax
import jax.numpy as jnp
import numpy as np
from jax import lax

QUERY_HEADS = 16
KEY_VALUE_HEADS = 4
HEAD_SIZE = 128
DOCUMENT_REACH = 8
T_DEV = 128
TILE_TOKENS = 64
MOST_DOC = 512
SEQUENCE_TOKENS = 2048
DOCS = 8


def draw_key_rows(key, part):
    gaussian_part = jax.random.normal(jax.random.fold_in(key, 21), (SEQUENCE_TOKENS, KEY_VALUE_HEADS * HEAD_SIZE), jnp.float32)
    return jnp.clip(gaussian_part, -4.0, 4.0).astype(jnp.bfloat16)


def draw_queries(key, part):
    gaussian_part = jax.random.normal(jax.random.fold_in(key, 31), (SEQUENCE_TOKENS, QUERY_HEADS * HEAD_SIZE), jnp.float32)
    return jnp.clip(gaussian_part, -4.0, 4.0).astype(jnp.bfloat16)


def steps_of(rng, shape, split, least, top_value):
    level = 1.0
    for axis_at, parts in split:
        steps = jax.random.uniform(jax.random.fold_in(jax.random.fold_in(rng, 6), axis_at), (parts,), jnp.float32, least / len(split), top_value / len(split))
        level = level * jnp.repeat(jnp.exp(steps), shape[axis_at] // parts).reshape((-1,) + (1,) * (len(shape) - 1 - axis_at))
    return level


def split_up(amount, total, bound, slope):
    portions = [(1 << 20) // math.isqrt(rank ** slope) + 1 for rank in range(2, amount + 1)]
    rest, holding = total - bound - (amount - 1), [1] * (amount - 1)
    while rest > 0:
        free = [i for i in range(amount - 1) if holding[i] < bound]
        pool, remaining = sum([portions[i] for i in free]), rest
        for i in free:
            extra = min(bound - holding[i], max(1, remaining * portions[i] // pool), rest)
            holding[i] = holding[i] + extra
            rest = rest - extra
    return np.array([bound] + holding)


def uneven_parts(rng, count, total, reach, skew):
    if count == 2:
        one = jax.random.randint(rng, (), max(1, total - reach), min(reach, total - 1) + 1)
        return jnp.stack([one, total - one])
    sizes = jnp.asarray(split_up(count, total, reach, skew), jnp.int32)
    pairs = (count - 1) // 2
    donor, taker = sizes[1:1 + 2 * pairs:2], sizes[2:2 + 2 * pairs:2]
    slack = jnp.minimum(donor - 1, reach - taker)
    moved = jax.random.randint(jax.random.fold_in(rng, 1), (pairs,), 0, 1 << 20) % (slack + 1)
    sizes = sizes.at[1:1 + 2 * pairs:2].set(donor - moved).at[2:2 + 2 * pairs:2].set(taker + moved)
    return sizes[jax.random.permutation(jax.random.fold_in(rng, 2), count)]


def normal_values(rng, dims, width, limit, pieces=(), kind=jnp.bfloat16):
    values = width * jax.random.normal(rng, dims, jnp.float32)
    if pieces:
        values = values * steps_of(rng, dims, pieces, -0.22, 0.18)
    return jnp.clip(values, -limit, limit).astype(kind)


def setup_inputs(seed: int = 0, part: int = 0) -> dict:
    key_list = jax.random.split(jax.random.key(seed), 6)
    part_keys = jax.random.split(jax.random.fold_in(key_list[5], part), 6)
    return {
        "queries": draw_queries(jax.random.fold_in(jax.random.fold_in(key_list[5], part), 71), part),
        "key_rows": draw_key_rows(jax.random.fold_in(jax.random.fold_in(key_list[5], part), 71), part),
        "value_rows": normal_values(part_keys[2], (SEQUENCE_TOKENS, KEY_VALUE_HEADS * HEAD_SIZE), 1.0, 6.0, ((0, 16),)),
        "output_gradient": normal_values(part_keys[3], (SEQUENCE_TOKENS, QUERY_HEADS * HEAD_SIZE), 1.0, 6.0, ((0, 16),)),
        "lengths": uneven_parts(part_keys[4], DOCS, SEQUENCE_TOKENS, MOST_DOC, 2).astype(jnp.int32),
    }


NEGATIVE_FLOOR = -1e+30

def row_positions(count, per_device, tile_rows):
    row_ids = jnp.arange(count, dtype=jnp.int32)
    device_id = row_ids // per_device
    within = row_ids % per_device
    block_id = jnp.where(within < tile_rows, device_id, count // tile_rows - 1 - device_id)
    return (block_id * tile_rows + within % tile_rows).astype(jnp.int32)

def doc_number(lengths, places):
    doc_ends = jnp.cumsum(lengths).astype(jnp.int32)
    doc_hits = (doc_ends[None, :] <= places[:, None]).astype(jnp.int32)
    return lax.optimization_barrier(jnp.sum(doc_hits, axis=1)).astype(jnp.int32)

def rounded(values):
    return lax.optimization_barrier(values.astype(jnp.bfloat16)).astype(jnp.float32)

def reference(queries, key_rows, value_rows, output_gradient, lengths):
    group_width = QUERY_HEADS // KEY_VALUE_HEADS
    tile_number_count = SEQUENCE_TOKENS // TILE_TOKENS
    score_scale = 1.0 / math.sqrt(HEAD_SIZE)
    highest = lax.Precision.HIGHEST
    row_location = row_positions(SEQUENCE_TOKENS, T_DEV, TILE_TOKENS)

    def into_positions(values, trailing):
        return jnp.zeros_like(values).at[row_location].set(values).reshape((tile_number_count, TILE_TOKENS) + trailing)
    query_sequence = into_positions(queries, (KEY_VALUE_HEADS, group_width, HEAD_SIZE))
    sequence_gradient = into_positions(output_gradient, (KEY_VALUE_HEADS, group_width, HEAD_SIZE))
    empty_blocks = jnp.zeros((DOCUMENT_REACH, TILE_TOKENS, KEY_VALUE_HEADS, HEAD_SIZE), key_rows.dtype)
    padded_keys = jnp.concatenate([empty_blocks, into_positions(key_rows, (KEY_VALUE_HEADS, HEAD_SIZE))], axis=0)
    padded_values = jnp.concatenate([empty_blocks, into_positions(value_rows, (KEY_VALUE_HEADS, HEAD_SIZE))], axis=0)
    offsets = jnp.arange(TILE_TOKENS, dtype=jnp.int32)
    zero_heads = jnp.zeros((TILE_TOKENS, KEY_VALUE_HEADS, group_width, HEAD_SIZE), jnp.float32)
    key_value_zeros = jnp.zeros((TILE_TOKENS, KEY_VALUE_HEADS, HEAD_SIZE), jnp.float32)

    def one_tile(carry, tile_id):
        key_gradient_part, value_gradient_part = carry
        query_tile_rows = lax.dynamic_index_in_dim(query_sequence, tile_id, 0, keepdims=False).astype(jnp.float32)
        tile_gradient = lax.dynamic_index_in_dim(sequence_gradient, tile_id, 0, keepdims=False).astype(jnp.float32)
        query_place = tile_id * TILE_TOKENS + offsets
        query_doc = doc_number(lengths, query_place)
        blocks = []
        for distance in range(DOCUMENT_REACH + 1):
            slot_id = tile_id + DOCUMENT_REACH - distance
            key_place = (tile_id - distance) * TILE_TOKENS + offsets
            key_doc = doc_number(lengths, key_place)
            visible = (query_doc[:, None] == key_doc[None, :]) & (key_place[None, :] <= query_place[:, None]) & (key_place[None, :] >= 0)
            key_tile = lax.dynamic_index_in_dim(padded_keys, slot_id, 0, keepdims=False).astype(jnp.float32)
            value_tile = lax.dynamic_index_in_dim(padded_values, slot_id, 0, keepdims=False).astype(jnp.float32)
            active = jnp.any(visible)

            def score_block(key_in=key_tile):
                return jnp.einsum('imgx,jmx->mgij', query_tile_rows, key_in, precision=highest) * score_scale

            def score_empty():
                return jnp.zeros((KEY_VALUE_HEADS, group_width, TILE_TOKENS, TILE_TOKENS), jnp.float32)
            raw_scores = lax.cond(active, score_block, score_empty)
            scores = jnp.where(visible, raw_scores, NEGATIVE_FLOOR)
            blocks.append((slot_id, visible, active, key_tile, value_tile, scores))
        row_maximum = lax.optimization_barrier(jnp.max(blocks[0][5], axis=-1))
        for block in blocks[1:]:
            row_maximum = jnp.maximum(row_maximum, lax.optimization_barrier(jnp.max(block[5], axis=-1)))
        row_total_sum = jnp.zeros_like(row_maximum)
        for block in blocks:
            row_total_sum = row_total_sum + lax.optimization_barrier(jnp.sum(jnp.where(block[1], jnp.exp(block[5] - row_maximum[..., None]), 0.0), axis=-1))
        log_norm = row_maximum + jnp.log(row_total_sum)
        attended = zero_heads
        for slot_id, visible, active, key_tile, value_tile, scores in blocks:

            def weigh_block(mask_in=visible, score_in=scores, value_in=value_tile):
                probs_b = rounded(jnp.where(mask_in, jnp.exp(score_in - log_norm[..., None]), 0.0))
                return jnp.einsum('mgij,jmx->imgx', probs_b, value_in, precision=highest)
            attended = attended + lax.cond(active, weigh_block, lambda: zero_heads)
        output_bf = rounded(attended)
        delta_dot = jnp.einsum('imgx,imgx->mgi', tile_gradient, output_bf, precision=highest)
        query_grad = zero_heads
        for slot_id, visible, active, key_tile, value_tile, scores in blocks:

            def tile_grads(mask_in=visible, score_in=scores, key_in=key_tile, value_in=value_tile):
                probs = jnp.where(mask_in, jnp.exp(score_in - log_norm[..., None]), 0.0)
                probs_b = rounded(probs)
                dprob = jnp.einsum('imgx,jmx->mgij', tile_gradient, value_in, precision=highest)
                dscore = rounded(probs * (dprob - delta_dot[..., None]))
                part_q = jnp.einsum('mgij,jmx->imgx', dscore, key_in, precision=highest) * score_scale
                part_k = jnp.einsum('mgij,imgx->jmx', dscore, query_tile_rows, precision=highest) * score_scale
                part_v = jnp.einsum('mgij,imgx->jmx', probs_b, tile_gradient, precision=highest)
                return (part_q, part_k, part_v)

            def no_grads():
                return (zero_heads, key_value_zeros, key_value_zeros)
            part_q, part_k, part_v = lax.cond(active, tile_grads, no_grads)
            query_grad = query_grad + part_q
            key_gradient_part = key_gradient_part.at[slot_id].add(part_k)
            value_gradient_part = value_gradient_part.at[slot_id].add(part_v)
        return ((key_gradient_part, value_gradient_part), (output_bf, query_grad))
    initial_gradients = jnp.zeros((tile_number_count + DOCUMENT_REACH, TILE_TOKENS, KEY_VALUE_HEADS, HEAD_SIZE), jnp.float32)
    carry, stacked = lax.scan(one_tile, (initial_gradients, initial_gradients), jnp.arange(tile_number_count, dtype=jnp.int32))
    key_gradient_part, value_gradient_part = carry
    output_seq, query_grad = stacked
    attended = output_seq.reshape(SEQUENCE_TOKENS, QUERY_HEADS * HEAD_SIZE)[row_location].astype(jnp.bfloat16)
    grad_queries = query_grad.reshape(SEQUENCE_TOKENS, QUERY_HEADS * HEAD_SIZE)[row_location].astype(jnp.bfloat16)
    key_gradient = key_gradient_part[DOCUMENT_REACH:].reshape(SEQUENCE_TOKENS, KEY_VALUE_HEADS * HEAD_SIZE)[row_location].astype(jnp.bfloat16)
    value_gradient = value_gradient_part[DOCUMENT_REACH:].reshape(SEQUENCE_TOKENS, KEY_VALUE_HEADS * HEAD_SIZE)[row_location].astype(jnp.bfloat16)
    return (attended, grad_queries, key_gradient, value_gradient)
```

```python
import functools
import math

import jax
import jax.numpy as jnp
from jax import lax
from jax.experimental import pallas as pl
from jax.experimental.pallas import tpu as pltpu
from jax.sharding import PartitionSpec as P

KV_HEADS = 4
HEAD = 128
GROUP = 4
HALF_HEADS = KV_HEADS // 2
PAIR = 128
BLOCK = 64
WINDOW = 5 * PAIR
WIDE = GROUP * HEAD
NEGATIVE_FLOOR = -1e30
SCALE = 1.0 / math.sqrt(HEAD)


def kernel(
    chips,
    lengths_ref,
    q_hbm,
    k_hbm,
    v_hbm,
    g_hbm,
    out_hbm,
    dq_hbm,
    dk_hbm,
    dv_hbm,
    qbuf,
    gbuf,
    kvbuf,
    obuf,
    dqbuf,
    kept,
    up_send,
    up_recv,
    sum_send,
    sum_recv,
    final,
    local_sem,
    swap_send,
    swap_recv,
    kv_send,
    kv_recv,
    grad_send,
    grad_recv,
    out_local,
    out_send,
    out_recv,
    fin_local,
    fin_send,
    fin_recv,
):
    ctx = lax.axis_index("ctx")
    chip = ctx // 2
    core = ctx - 2 * chip
    other = 1 - core
    sibling = 2 * chip + other
    last = 2 * chips - 1

    def place(side):
        return chip + side * (last - 2 * chip)

    def half_of(side, core_id):
        return core_id + side * (1 - 2 * core_id)

    def owner(t):
        return jnp.where(t < chips, t, last - t)

    def side_of(t):
        return jnp.where(t < chips, 0, 1)

    def remote(src, dst, send, recv, device):
        return pltpu.make_async_remote_copy(
            src_ref=src,
            dst_ref=dst,
            send_sem=send,
            recv_sem=recv,
            device_id={"ctx": device},
            device_id_type=pl.DeviceIdType.MESH,
        )

    @pl.when(chip < 2)
    def _():
        for h in range(HALF_HEADS):
            kvbuf[0, h, 0 : 4 * PAIR, :] = jnp.zeros((4 * PAIR, 2 * HEAD), jnp.bfloat16)

    barrier = pltpu.get_barrier_semaphore()
    pl.semaphore_signal(
        barrier, inc=1, device_id={"ctx": sibling}, device_id_type=pl.DeviceIdType.MESH
    )
    for step in (-2, -1, 1, 2):
        peer = chip + step

        @pl.when((peer >= 0) & (peer < chips))
        def _():
            pl.semaphore_signal(
                barrier,
                inc=1,
                device_id={"ctx": 2 * peer + core},
                device_id_type=pl.DeviceIdType.MESH,
            )

    count = 1
    for step in (-2, -1, 1, 2):
        peer = chip + step
        count = count + jnp.where((peer >= 0) & (peer < chips), 1, 0)
    pl.semaphore_wait(barrier, count)

    def kv_stage(s, h, x, who):
        src = (k_hbm, v_hbm)[x].at[
            pl.ds(s * BLOCK, BLOCK), pl.ds(pl.multiple_of((who * HALF_HEADS + h) * HEAD, HEAD), HEAD)
        ]
        rows = pl.multiple_of(4 * PAIR + half_of(s, core) * BLOCK, BLOCK)
        dst = kvbuf.at[s, h, pl.ds(rows, BLOCK), pl.ds(x * HEAD, HEAD)]
        return src, dst

    def q_stage(s, h, x, who):
        src = (q_hbm, g_hbm)[x].at[
            pl.ds(s * BLOCK, BLOCK), pl.ds(pl.multiple_of((who * HALF_HEADS + h) * WIDE, WIDE), WIDE)
        ]
        rows = pl.multiple_of(half_of(s, core) * BLOCK, BLOCK)
        dst = (qbuf, gbuf)[x].at[s, h, pl.ds(rows, BLOCK), :]
        return src, dst

    def staged(kind, s, h, x):
        stage = (kv_stage, q_stage)[kind]
        src, dst = stage(s, h, x, core)
        mine = pltpu.make_async_copy(src, dst, local_sem.at[kind, s, h, x])
        src, dst = stage(s, h, x, other)
        swap = remote(
            src, dst, swap_send.at[kind, s, h, x], swap_recv.at[kind, s, h, x], sibling
        )
        return mine, swap

    order = [(s, h, x) for h in range(HALF_HEADS) for s in range(2) for x in range(2)]
    for kind in range(2):
        for s, h, x in order:
            mine, swap = staged(kind, s, h, x)
            swap.start()
            mine.start()

    def forward(s, h, step):
        t = place(s) + step
        rows = (4 - step) * PAIR
        src = kvbuf.at[s, h, pl.ds(4 * PAIR, PAIR), :]
        dst = kvbuf.at[side_of(t), h, pl.ds(rows, PAIR), :]
        return t, remote(
            src,
            dst,
            kv_send.at[s, h, step - 1],
            kv_recv.at[side_of(t), h, step - 1],
            2 * owner(t) + core,
        )

    def forward_self(h):
        return pltpu.make_async_copy(
            kvbuf.at[0, h, pl.ds(4 * PAIR, PAIR), :],
            kvbuf.at[1, h, pl.ds(3 * PAIR, PAIR), :],
            kv_recv.at[1, h, 0],
        )

    def relay(s, h):
        t = place(s) + 2
        return t, remote(
            kvbuf.at[s, h, pl.ds(2 * PAIR, 2 * PAIR), :],
            kvbuf.at[side_of(t), h, pl.ds(0, 2 * PAIR), :],
            kv_send.at[s, h, 2],
            kv_recv.at[side_of(t), h, 2],
            2 * owner(t) + core,
        )

    def arrived(s, h, kind):
        rows = ((3, 1), (2, 1), (0, 2))[kind]
        ref = kvbuf.at[s, h, pl.ds(rows[0] * PAIR, rows[1] * PAIR), :]
        return remote(ref, ref, kv_send.at[s, h, kind], kv_recv.at[s, h, kind], sibling)

    for h in range(HALF_HEADS):
        for s in range(2):
            for x in range(2):
                mine, swap = staged(0, s, h, x)
                mine.wait()
                swap.wait_recv()
            t, copy = forward(s, h, 2)
            pl.when(t <= last)(copy.start)
            t, copy = forward(s, h, 1)
            if s == 0:
                pl.when(chip < chips - 1)(copy.start)
                pl.when(chip == chips - 1)(forward_self(h).start)
            else:
                pl.when(t <= last)(copy.start)

    for h in range(HALF_HEADS):
        for s in range(2):
            here = place(s)
            pl.when(here >= 1)(arrived(s, h, 0).wait_recv)
            pl.when(here >= 2)(arrived(s, h, 1).wait_recv)
            t, copy = relay(s, h)
            pl.when(t <= last)(copy.start)

    def out_copies(s, h, x):
        buf = (obuf, dqbuf)[x]
        hbm = (out_hbm, dq_hbm)[x]
        columns = pl.ds(pl.multiple_of((core * HALF_HEADS + h) * WIDE, WIDE), WIDE)
        rows = pl.ds(pl.multiple_of(s * BLOCK, BLOCK), BLOCK)
        own = pl.ds(pl.multiple_of(half_of(s, core) * BLOCK, BLOCK), BLOCK)
        theirs = pl.ds(pl.multiple_of(half_of(s, other) * BLOCK, BLOCK), BLOCK)
        mine = pltpu.make_async_copy(
            buf.at[s, h, own, :], hbm.at[rows, columns], out_local.at[s, h, x]
        )
        swap = remote(
            buf.at[s, h, theirs, :],
            hbm.at[rows, columns],
            out_send.at[s, h, x],
            out_recv.at[s, h, x],
            sibling,
        )
        return mine, swap

    def partial_up(s, h):
        t = place(s) - 2
        return t, remote(
            up_send.at[s, h],
            up_recv.at[side_of(t), h],
            grad_send.at[s, h, 2],
            grad_recv.at[side_of(t), h, 2],
            2 * owner(t) + core,
        )

    def summed(s, h, step):
        t = place(s) - step
        rows = pl.ds((2 - step) * PAIR, PAIR)
        return t, remote(
            sum_send.at[s, h, rows, :],
            sum_recv.at[side_of(t), h, step - 1],
            grad_send.at[s, h, step - 1],
            grad_recv.at[side_of(t), h, step - 1],
            2 * owner(t) + core,
        )

    def summed_self(h):
        return pltpu.make_async_copy(
            sum_send.at[1, h, pl.ds(PAIR, PAIR), :],
            sum_recv.at[0, h, 0],
            grad_recv.at[0, h, 0],
        )

    def grad_arrived(s, h, kind):
        ref = up_recv.at[s, h] if kind == 2 else sum_recv.at[s, h, kind]
        return remote(ref, ref, grad_send.at[s, h, kind], grad_recv.at[s, h, kind], sibling)

    def compute(s, h):
        here = place(s)
        for x in range(2):
            mine, swap = staged(1, s, h, x)
            mine.wait()
            swap.wait_recv()
        pl.when(here >= 2)(arrived(s, h, 2).wait_recv)

        query_at = here * PAIR + lax.broadcasted_iota(jnp.int32, (1, PAIR), 1)
        start = jnp.zeros((1, PAIR), jnp.int32)
        end = jnp.int32(0)
        for doc in range(lengths_ref.shape[0]):
            end = end + lengths_ref[doc]
            start = jnp.maximum(start, jnp.where(end <= query_at, end, 0))
        key_at = (here - 4) * PAIR + lax.broadcasted_iota(jnp.int32, (WINDOW, PAIR), 0)
        visible = (key_at >= start) & (key_at <= query_at)
        bias = jnp.where(visible, 0.0, NEGATIVE_FLOOR).astype(jnp.float32)
        bias = jnp.concatenate([bias] * GROUP, axis=1)

        keys = kvbuf[s, h, :, 0:HEAD]
        values = kvbuf[s, h, :, HEAD : 2 * HEAD]
        q = jnp.concatenate(
            [qbuf[s, h, :, g * HEAD : (g + 1) * HEAD] for g in range(GROUP)], axis=0
        )
        grad = jnp.concatenate(
            [gbuf[s, h, :, g * HEAD : (g + 1) * HEAD] for g in range(GROUP)], axis=0
        )
        grad_t = grad.T
        scores = lax.dot_general(
            keys, q, (((1,), (1,)), ((), ())), preferred_element_type=jnp.float32
        )
        scores = scores + bias
        top = jnp.max(scores, axis=0, keepdims=True)
        weights = jnp.exp2((scores - top) * (SCALE * math.log2(math.e)))
        total = jnp.sum(weights, axis=0, keepdims=True)
        probs = weights * (1.0 / total)
        probs_b = probs.astype(jnp.bfloat16)
        attended_t = jnp.dot(values.T, probs_b, preferred_element_type=jnp.float32)
        attended_b = attended_t.astype(jnp.bfloat16)
        delta = jnp.sum(
            attended_b.astype(jnp.float32) * grad_t.astype(jnp.float32), axis=0, keepdims=True
        )
        dprob = jnp.dot(values, grad_t, preferred_element_type=jnp.float32)
        dscore = (probs * (dprob - delta)).astype(jnp.bfloat16)
        dq_t = jnp.dot(keys.T, dscore, preferred_element_type=jnp.float32) * SCALE
        dk = jnp.dot(dscore, q, preferred_element_type=jnp.float32) * SCALE
        dv = jnp.dot(probs_b, grad, preferred_element_type=jnp.float32)
        attended = attended_b.T
        dq = dq_t.astype(jnp.bfloat16).T
        for g in range(GROUP):
            obuf[s, h, :, g * HEAD : (g + 1) * HEAD] = attended[g * PAIR : (g + 1) * PAIR]
            dqbuf[s, h, :, g * HEAD : (g + 1) * HEAD] = dq[g * PAIR : (g + 1) * PAIR]
        up_send[s, h, :, 0:HEAD] = dk[0 : 2 * PAIR].astype(jnp.bfloat16)
        up_send[s, h, :, HEAD : 2 * HEAD] = dv[0 : 2 * PAIR].astype(jnp.bfloat16)
        t, copy = partial_up(s, h)
        pl.when(t >= 0)(copy.start)
        kept[s, h, :, 0:HEAD] = dk[2 * PAIR :]
        kept[s, h, :, HEAD : 2 * HEAD] = dv[2 * PAIR :]
        for x in range(2):
            mine, swap = out_copies(s, h, x)
            swap.start()
            mine.start()

    def pass_down(s, h):
        here = place(s)
        more = here + 2 <= last

        @pl.when(more)
        def _():
            grad_arrived(s, h, 2).wait_recv()
            sum_send[s, h] = (
                kept[s, h, 0 : 2 * PAIR, :] + up_recv[s, h].astype(jnp.float32)
            ).astype(jnp.bfloat16)

        @pl.when(jnp.logical_not(more))
        def _():
            sum_send[s, h] = kept[s, h, 0 : 2 * PAIR, :].astype(jnp.bfloat16)

        t, copy = summed(s, h, 2)
        pl.when(t >= 0)(copy.start)
        t, copy = summed(s, h, 1)
        at_self = here == chips
        pl.when((t >= 0) & jnp.logical_not(at_self))(copy.start)
        pl.when(at_self)(summed_self(h).start)

    def fin_copies(s, h, x):
        hbm = (dk_hbm, dv_hbm)[x]
        columns = pl.ds(pl.multiple_of((core * HALF_HEADS + h) * HEAD, HEAD), HEAD)
        rows = pl.ds(pl.multiple_of(s * BLOCK, BLOCK), BLOCK)
        own = pl.ds(pl.multiple_of(half_of(s, core) * BLOCK, BLOCK), BLOCK)
        theirs = pl.ds(pl.multiple_of(half_of(s, other) * BLOCK, BLOCK), BLOCK)
        cut = pl.ds(x * HEAD, HEAD)
        mine = pltpu.make_async_copy(
            final.at[s, h, own, cut], hbm.at[rows, columns], fin_local.at[s, h, x]
        )
        swap = remote(
            final.at[s, h, theirs, cut],
            hbm.at[rows, columns],
            fin_send.at[s, h, x],
            fin_recv.at[s, h, x],
            sibling,
        )
        return mine, swap

    def finish(s, h):
        here = place(s)
        for step in (1, 2):

            @pl.when(here + step <= last)
            def _():
                grad_arrived(s, h, step - 1).wait_recv()
                kept[s, h, 2 * PAIR :, :] += sum_recv[s, h, step - 1].astype(jnp.float32)

        final[s, h] = kept[s, h, 2 * PAIR :, :].astype(jnp.bfloat16)
        for x in range(2):
            mine, swap = fin_copies(s, h, x)
            swap.start()
            mine.start()

    def turn(i, carry):
        compute(lax.rem(i, 2), i // 2)

        @pl.when(i >= 2)
        def _():
            pass_down(lax.rem(i, 2), i // 2 - 1)

        return carry

    lax.fori_loop(0, 4, turn, 0)
    for s in range(2):
        pass_down(s, 1)
    for h in range(HALF_HEADS):
        for s in range(2):
            finish(s, h)

    for h in range(HALF_HEADS):
        for s in range(2):
            here = place(s)
            for x in range(2):
                for kind in range(2):
                    mine, swap = staged(kind, s, h, x)
                    swap.wait_send()
                for copies in (out_copies, fin_copies):
                    mine, swap = copies(s, h, x)
                    mine.wait()
                    swap.wait_send()
                    swap.wait_recv()
            t, copy = forward(s, h, 2)
            pl.when(t <= last)(copy.wait_send)
            t, copy = forward(s, h, 1)
            pl.when((t <= last) & (here != chips - 1))(copy.wait_send)
            t, copy = relay(s, h)
            pl.when(t <= last)(copy.wait_send)
            t, copy = partial_up(s, h)
            pl.when(t >= 0)(copy.wait_send)
            t, copy = summed(s, h, 2)
            pl.when(t >= 0)(copy.wait_send)
            t, copy = summed(s, h, 1)
            pl.when((t >= 0) & (here != chips))(copy.wait_send)


def on_device(queries, key_rows, value_rows, output_gradient, lengths):
    chips = lax.axis_size("ctx") // 2
    anywhere = pl.BlockSpec(memory_space=pl.ANY)
    bf16 = jnp.bfloat16
    dma = pltpu.SemaphoreType.DMA
    scratch = [
        pltpu.VMEM((2, 2, PAIR, WIDE), bf16),
        pltpu.VMEM((2, 2, PAIR, WIDE), bf16),
        pltpu.VMEM((2, 2, WINDOW, 2 * HEAD), bf16),
        pltpu.VMEM((2, 2, PAIR, WIDE), bf16),
        pltpu.VMEM((2, 2, PAIR, WIDE), bf16),
        pltpu.VMEM((2, 2, 3 * PAIR, 2 * HEAD), jnp.float32),
        pltpu.VMEM((2, 2, 2 * PAIR, 2 * HEAD), bf16),
        pltpu.VMEM((2, 2, 2 * PAIR, 2 * HEAD), bf16),
        pltpu.VMEM((2, 2, 2 * PAIR, 2 * HEAD), bf16),
        pltpu.VMEM((2, 2, 2, PAIR, 2 * HEAD), bf16),
        pltpu.VMEM((2, 2, PAIR, 2 * HEAD), bf16),
        dma((2, 2, 2, 2)),
        dma((2, 2, 2, 2)),
        dma((2, 2, 2, 2)),
        dma((2, 2, 3)),
        dma((2, 2, 3)),
        dma((2, 2, 3)),
        dma((2, 2, 3)),
    ] + [dma((2, 2, 2)) for _ in range(6)]
    return pl.pallas_call(
        functools.partial(kernel, chips),
        out_shape=tuple(
            jax.ShapeDtypeStruct(a.shape, bf16)
            for a in (queries, queries, key_rows, value_rows)
        ),
        in_specs=[pl.BlockSpec(memory_space=pltpu.SMEM)] + [anywhere] * 4,
        out_specs=(anywhere,) * 4,
        scratch_shapes=scratch,
        compiler_params=pltpu.CompilerParams(
            collective_id=0, has_side_effects=True, vmem_limit_bytes=40 * 1024 * 1024
        ),
    )(lengths, queries, key_rows, value_rows, output_gradient)


def solution(mesh):
    rows = P(("groups", "ctx"), None)
    return jax.shard_map(
        on_device,
        mesh=mesh,
        in_specs=(rows, rows, rows, rows, P("groups")),
        out_specs=(rows, rows, rows, rows),
        check_vma=False,
    )
```

```python
import functools
import math

import jax
import jax.numpy as jnp
from jax import lax
from jax.experimental import pallas as pl
from jax.experimental.pallas import tpu as pltpu
from jax.sharding import PartitionSpec as P

KV_HEADS = 4
HEAD = 128
GROUP = 4
HALF_HEADS = KV_HEADS // 2
PAIR = 128
BLOCK = 64
WINDOW = 5 * PAIR
WIDE = GROUP * HEAD
NEGATIVE_FLOOR = -1e30
SCALE = 1.0 / math.sqrt(HEAD)


def kernel(
    chips,
    lengths_ref,
    q_hbm,
    k_hbm,
    v_hbm,
    g_hbm,
    packed,
    qbuf,
    gbuf,
    kvbuf,
    obuf,
    dqbuf,
    kept,
    up_send,
    up_recv,
    sum_send,
    sum_recv,
    final,
    local_sem,
    swap_send,
    swap_recv,
    kv_send,
    kv_recv,
    grad_send,
    grad_recv,
    out_local,
    out_send,
    out_recv,
    fin_local,
    fin_send,
    fin_recv,
):
    ctx = lax.axis_index("ctx")
    chip = ctx // 2
    core = ctx - 2 * chip
    other = 1 - core
    sibling = 2 * chip + other
    last = 2 * chips - 1

    def place(side):
        return chip + side * (last - 2 * chip)

    def half_of(side, core_id):
        return core_id + side * (1 - 2 * core_id)

    def owner(t):
        return jnp.where(t < chips, t, last - t)

    def side_of(t):
        return jnp.where(t < chips, 0, 1)

    def remote(src, dst, send, recv, device):
        return pltpu.make_async_remote_copy(
            src_ref=src,
            dst_ref=dst,
            send_sem=send,
            recv_sem=recv,
            device_id={"ctx": device},
            device_id_type=pl.DeviceIdType.MESH,
        )

    partner = 2 * (chip + 1 - 2 * lax.rem(chip, 2)) + core

    def odd(s):
        return lax.rem(place(s), 2) == 1

    for slot in range(4):

        @pl.when(chip + slot < 4)
        def _():
            for h in range(HALF_HEADS):
                kvbuf[0, h, slot * PAIR : (slot + 1) * PAIR, :] = jnp.zeros(
                    (PAIR, 2 * HEAD), jnp.bfloat16
                )

    barrier = pltpu.get_barrier_semaphore()
    for device in (sibling, partner):
        pl.semaphore_signal(
            barrier, inc=1, device_id={"ctx": device}, device_id_type=pl.DeviceIdType.MESH
        )
    count = 2
    for step in (-2, 2):
        peer = chip + step
        near = (peer >= 0) & (peer < chips)

        @pl.when(near)
        def _():
            pl.semaphore_signal(
                barrier,
                inc=1,
                device_id={"ctx": 2 * peer + core},
                device_id_type=pl.DeviceIdType.MESH,
            )

        count = count + jnp.where(near, 1, 0)
    pl.semaphore_wait(barrier, count)

    def kv_stage(s, h, x, who):
        src = (k_hbm, v_hbm)[x].at[
            pl.ds(s * BLOCK, BLOCK), pl.ds(pl.multiple_of((who * HALF_HEADS + h) * HEAD, HEAD), HEAD)
        ]
        rows = pl.multiple_of(4 * PAIR + half_of(s, core) * BLOCK, BLOCK)
        dst = kvbuf.at[s, h, pl.ds(rows, BLOCK), pl.ds(x * HEAD, HEAD)]
        return src, dst

    def q_stage(s, h, x, who):
        src = (q_hbm, g_hbm)[x].at[
            pl.ds(s * BLOCK, BLOCK), pl.ds(pl.multiple_of((who * HALF_HEADS + h) * WIDE, WIDE), WIDE)
        ]
        rows = pl.multiple_of(half_of(s, core) * BLOCK, BLOCK)
        dst = (qbuf, gbuf)[x].at[s, h, pl.ds(rows, BLOCK), :]
        return src, dst

    def staged_mine(kind, s, h, x):
        src, dst = (kv_stage, q_stage)[kind](s, h, x, core)
        return pltpu.make_async_copy(src, dst, local_sem.at[kind, s, h, x])

    def staged_swap(kind, s, h, x):
        src, dst = (kv_stage, q_stage)[kind](s, h, x, other)
        return remote(
            src, dst, swap_send.at[kind, s, h, x], swap_recv.at[kind, s, h, x], sibling
        )

    order = [(s, h, x) for h in range(HALF_HEADS) for s in range(2) for x in range(2)]
    for kind in range(2):
        for s, h, x in order:
            staged_swap(kind, s, h, x).start()
            staged_mine(kind, s, h, x).start()

    def rows_of(slot):
        return pl.ds(slot * PAIR, PAIR)

    def forward(s, h, kind):
        t = place(s) + 2
        source, target = ((4, 3), (4, 2), (2, 0), (3, 1))[kind]
        return remote(
            kvbuf.at[s, h, rows_of(source), :],
            kvbuf.at[side_of(t), h, rows_of(target), :],
            kv_send.at[s, h, kind],
            kv_recv.at[side_of(t), h, kind],
            2 * owner(t) + core,
        )

    def across(s, h, source):
        return remote(
            kvbuf.at[s, h, rows_of(source), :],
            kvbuf.at[s, h, rows_of(3), :],
            kv_send.at[s, h, 0],
            kv_recv.at[s, h, 0],
            partner,
        )

    def arrived(s, h, kind):
        ref = kvbuf.at[s, h, rows_of((3, 2, 0, 1)[kind]), :]
        return remote(ref, ref, kv_send.at[s, h, kind], kv_recv.at[s, h, kind], sibling)

    def sends_own(t):
        return (t + 2 <= last) & (t + 2 != chips)

    def sends_relay(t):
        return sends_own(t) & (t + 2 != chips + 1)

    def odd_across(t):
        return (lax.rem(t, 2) == 1) & (t >= 3) & (t != chips + 1)

    def even_across(t):
        return (lax.rem(t, 2) == 0) & (t >= 2) & (t != chips)

    for h in range(HALF_HEADS):
        for s in range(2):
            here = place(s)
            for x in range(2):
                staged_mine(0, s, h, x).wait()
                staged_swap(0, s, h, x).wait_recv()
            pl.when(sends_own(here))(forward(s, h, 1).start)
            pl.when(jnp.logical_not(odd(s)))(across(s, h, 4).start)

    for h in range(HALF_HEADS):
        for s in range(2):
            here = place(s)
            pl.when((here >= 2) & (here != chips))(arrived(s, h, 1).wait_recv)
            pl.when(odd_across(here))(across(s, h, 2).start)
            pl.when((here >= 2) & (here != chips) & sends_relay(here))(forward(s, h, 2).start)

    for h in range(HALF_HEADS):
        for s in range(2):
            here = place(s)
            pl.when(odd(s) | even_across(here))(arrived(s, h, 0).wait_recv)
            if s == 1:

                @pl.when(here == chips)
                def _():
                    kvbuf[1, h, 2 * PAIR : 4 * PAIR, :] = kvbuf[0, h, 3 * PAIR : 5 * PAIR, :]
                    forward(1, h, 2).start()

            pl.when((here >= 1) & sends_relay(here))(forward(s, h, 3).start)

    def out_place(s, h, x):
        columns = pl.ds(
            pl.multiple_of(x * KV_HEADS * WIDE + (core * HALF_HEADS + h) * WIDE, WIDE), WIDE
        )
        return packed.at[pl.ds(pl.multiple_of(s * BLOCK, BLOCK), BLOCK), columns]

    def fin_place(s, h, x):
        start = 2 * KV_HEADS * WIDE + x * KV_HEADS * HEAD
        columns = pl.ds(pl.multiple_of(start + (core * HALF_HEADS + h) * HEAD, HEAD), HEAD)
        return packed.at[pl.ds(pl.multiple_of(s * BLOCK, BLOCK), BLOCK), columns]

    def half_rows(s, who):
        return pl.ds(pl.multiple_of(half_of(s, who) * BLOCK, BLOCK), BLOCK)

    def out_mine(s, h, x):
        src = (obuf, dqbuf)[x].at[s, h, half_rows(s, core), :]
        return pltpu.make_async_copy(src, out_place(s, h, x), out_local.at[s, h, x])

    def out_swap(s, h, x):
        src = (obuf, dqbuf)[x].at[s, h, half_rows(s, other), :]
        return remote(
            src, out_place(s, h, x), out_send.at[s, h, x], out_recv.at[s, h, x], sibling
        )

    def fin_mine(s, h, x):
        src = final.at[s, h, half_rows(s, core), pl.ds(x * HEAD, HEAD)]
        return pltpu.make_async_copy(src, fin_place(s, h, x), fin_local.at[s, h, x])

    def fin_swap(s, h, x):
        src = final.at[s, h, half_rows(s, other), pl.ds(x * HEAD, HEAD)]
        return remote(
            src, fin_place(s, h, x), fin_send.at[s, h, x], fin_recv.at[s, h, x], sibling
        )

    def partial_up(s, h):
        t = place(s) - 2
        return remote(
            up_send.at[s, h],
            up_recv.at[side_of(t), h],
            grad_send.at[s, h, 2],
            grad_recv.at[side_of(t), h, 2],
            2 * owner(t) + core,
        )

    def summed_back(s, h):
        t = place(s) - 2
        return remote(
            sum_send.at[s, h, pl.ds(0, PAIR), :],
            sum_recv.at[side_of(t), h, 1],
            grad_send.at[s, h, 1],
            grad_recv.at[side_of(t), h, 1],
            2 * owner(t) + core,
        )

    def summed_across(s, h):
        return remote(
            sum_send.at[s, h, pl.ds(PAIR, PAIR), :],
            sum_recv.at[s, h, 0],
            grad_send.at[s, h, 0],
            grad_recv.at[s, h, 0],
            partner,
        )

    def grad_arrived(s, h, kind):
        ref = up_recv.at[s, h] if kind == 2 else sum_recv.at[s, h, kind]
        return remote(ref, ref, grad_send.at[s, h, kind], grad_recv.at[s, h, kind], sibling)

    def sends_up(t):
        return (t >= 2) & (t != chips) & (t != chips + 1)

    def sends_back(t):
        return (t >= 2) & (t != chips)

    def compute(s, h):
        here = place(s)
        for x in range(2):
            staged_mine(1, s, h, x).wait()
            staged_swap(1, s, h, x).wait_recv()
        relayed = (here != chips) & (here != chips + 1)
        relayed = relayed & jnp.logical_not((s == 0) & (chip == chips - 1))
        pl.when((here >= 4) & relayed)(arrived(s, h, 2).wait_recv)
        pl.when((here >= 3) & relayed)(arrived(s, h, 3).wait_recv)


        query_at = here * PAIR + lax.broadcasted_iota(jnp.int32, (1, PAIR), 1)
        start = jnp.zeros((1, PAIR), jnp.int32)
        end = jnp.int32(0)
        for doc in range(lengths_ref.shape[0]):
            end = end + lengths_ref[doc]
            start = jnp.maximum(start, jnp.where(end <= query_at, end, 0))
        key_at = (here - 4) * PAIR + lax.broadcasted_iota(jnp.int32, (WINDOW, PAIR), 0)
        visible = (key_at >= start) & (key_at <= query_at)
        bias = jnp.where(visible, 0.0, NEGATIVE_FLOOR).astype(jnp.float32)
        bias = jnp.concatenate([bias] * GROUP, axis=1)

        @pl.when(here == chips)
        def _():
            before = place(0)
            pl.when(before >= 4)(arrived(0, h, 2).wait_recv)
            pl.when(before >= 3)(arrived(0, h, 3).wait_recv)
            kvbuf[1, h, 0 : 2 * PAIR, :] = kvbuf[0, h, PAIR : 3 * PAIR, :]

        @pl.when(here == chips + 1)
        def _():
            kvbuf[1, h, 0 : 2 * PAIR, :] = kvbuf[0, h, 3 * PAIR : 5 * PAIR, :]

        keys = kvbuf[s, h, :, 0:HEAD]
        values = kvbuf[s, h, :, HEAD : 2 * HEAD]
        q = jnp.concatenate(
            [qbuf[s, h, :, g * HEAD : (g + 1) * HEAD] for g in range(GROUP)], axis=0
        )
        grad = jnp.concatenate(
            [gbuf[s, h, :, g * HEAD : (g + 1) * HEAD] for g in range(GROUP)], axis=0
        )
        grad_t = grad.T
        scores = lax.dot_general(
            keys, q, (((1,), (1,)), ((), ())), preferred_element_type=jnp.float32
        )
        scores = scores + bias
        top = jnp.max(scores, axis=0, keepdims=True)
        weights = jnp.exp2((scores - top) * (SCALE * math.log2(math.e)))
        total = jnp.sum(weights, axis=0, keepdims=True)
        probs = weights * (1.0 / total)
        probs_b = probs.astype(jnp.bfloat16)
        attended_t = jnp.dot(values.T, probs_b, preferred_element_type=jnp.float32)
        attended_b = attended_t.astype(jnp.bfloat16)
        delta = jnp.sum(
            attended_b.astype(jnp.float32) * grad_t.astype(jnp.float32), axis=0, keepdims=True
        )
        dprob = jnp.dot(values, grad_t, preferred_element_type=jnp.float32)
        dscore = (probs * (dprob - delta)).astype(jnp.bfloat16)
        dq_t = jnp.dot(keys.T, dscore, preferred_element_type=jnp.float32) * SCALE
        dk = jnp.dot(dscore, q, preferred_element_type=jnp.float32) * SCALE
        dv = jnp.dot(probs_b, grad, preferred_element_type=jnp.float32)
        attended = attended_b.T
        dq = dq_t.astype(jnp.bfloat16).T
        for g in range(GROUP):
            obuf[s, h, :, g * HEAD : (g + 1) * HEAD] = attended[g * PAIR : (g + 1) * PAIR]
            dqbuf[s, h, :, g * HEAD : (g + 1) * HEAD] = dq[g * PAIR : (g + 1) * PAIR]
        up_send[s, h, :, 0:HEAD] = dk[0 : 2 * PAIR].astype(jnp.bfloat16)
        up_send[s, h, :, HEAD : 2 * HEAD] = dv[0 : 2 * PAIR].astype(jnp.bfloat16)
        kept[s, h, :, 0:HEAD] = dk[2 * PAIR :]
        kept[s, h, :, HEAD : 2 * HEAD] = dv[2 * PAIR :]

        @pl.when((s == 0) & (chip == chips - 1))
        def _():
            up_send[0, h, PAIR:, :] += up_send[1, h, 0:PAIR, :]
            kept[0, h, 0:PAIR, :] += up_send[1, h, PAIR:, :].astype(jnp.float32)

        @pl.when((s == 0) & (chip == chips - 2))
        def _():
            kept[0, h, PAIR:, :] += up_send[1, h].astype(jnp.float32)

        pl.when(sends_up(here))(partial_up(s, h).start)
        for x in range(2):
            out_swap(s, h, x).start()
            out_mine(s, h, x).start()

    def pass_down(s, h):
        here = place(s)

        @pl.when(sends_relay(here))
        def _():
            grad_arrived(s, h, 2).wait_recv()
            kept[s, h, 0 : 2 * PAIR, :] += up_recv[s, h].astype(jnp.float32)

        @pl.when(here == chips)
        def _():
            kept[0, h, PAIR:, :] += kept[1, h, 0 : 2 * PAIR, :]

        sum_send[s, h, PAIR:, :] = kept[s, h, PAIR : 2 * PAIR, :].astype(jnp.bfloat16)
        pl.when(odd(s) | even_across(here))(summed_across(s, h).start)

        @pl.when(jnp.logical_not(odd(s)))
        def _():
            sum_send[s, h, 0:PAIR, :] = kept[s, h, 0:PAIR, :].astype(jnp.bfloat16)
            pl.when(sends_back(here))(summed_back(s, h).start)

    def pass_odd(s, h):
        here = place(s)

        @pl.when(odd(s))
        def _():
            @pl.when(odd_across(here))
            def _():
                grad_arrived(s, h, 0).wait_recv()
                kept[s, h, 0:PAIR, :] += sum_recv[s, h, 0].astype(jnp.float32)

            sum_send[s, h, 0:PAIR, :] = kept[s, h, 0:PAIR, :].astype(jnp.bfloat16)
            pl.when(sends_back(here))(summed_back(s, h).start)

    def finish(s, h):
        here = place(s)

        @pl.when(jnp.logical_not(odd(s)))
        def _():
            grad_arrived(s, h, 0).wait_recv()
            kept[s, h, 2 * PAIR :, :] += sum_recv[s, h, 0].astype(jnp.float32)

        @pl.when(sends_own(here))
        def _():
            grad_arrived(s, h, 1).wait_recv()
            kept[s, h, 2 * PAIR :, :] += sum_recv[s, h, 1].astype(jnp.float32)

        final[s, h] = kept[s, h, 2 * PAIR :, :].astype(jnp.bfloat16)
        for x in range(2):
            fin_swap(s, h, x).start()
            fin_mine(s, h, x).start()

    def turn(i, carry):
        side = 1 - lax.rem(i, 2)
        half = i // 2

        compute(side, half)

        @pl.when(i >= 2)
        def _():
            pass_down(side, half - 1)

        return carry

    lax.fori_loop(0, 4, turn, 0)
    for s in range(2):
        pass_odd(s, 0)
    for s in (1, 0):
        pass_down(s, 1)
    for s in range(2):
        pass_odd(s, 1)
    for h in range(HALF_HEADS):
        for s in range(2):
            finish(s, h)

    for h in range(HALF_HEADS):
        for s in range(2):
            here = place(s)
            for x in range(2):
                for kind in range(2):
                    staged_swap(kind, s, h, x).wait_send()
                out_mine(s, h, x).wait()
                fin_mine(s, h, x).wait()
                for swap in (out_swap, fin_swap):
                    swap(s, h, x).wait_send()
                    swap(s, h, x).wait_recv()
            pl.when(sends_own(here))(forward(s, h, 1).wait_send)
            pl.when(jnp.logical_not(odd(s)) | odd_across(here))(across(s, h, 4).wait_send)
            pl.when((here >= 2) & sends_relay(here))(forward(s, h, 2).wait_send)
            pl.when((here >= 1) & sends_relay(here))(forward(s, h, 3).wait_send)
            pl.when(sends_up(here))(partial_up(s, h).wait_send)
            pl.when(odd(s) | even_across(here))(summed_across(s, h).wait_send)
            pl.when(sends_back(here))(summed_back(s, h).wait_send)


def split_kernel(packed, out, dq, dk, dv, b0, b1, b2, b3, sem):
    ins, outs = [], []
    start = 0
    for i, (ref, buf) in enumerate(zip((out, dq, dk, dv), (b0, b1, b2, b3))):
        width = ref.shape[1]
        ins.append(pltpu.make_async_copy(packed.at[:, pl.ds(start, width)], buf, sem.at[0, i]))
        outs.append(pltpu.make_async_copy(buf, ref, sem.at[1, i]))
        start += width
    for copy in ins:
        copy.start()
    for a, b in zip(ins, outs):
        a.wait()
        b.start()
    for copy in outs:
        copy.wait()


def on_device(queries, key_rows, value_rows, output_gradient, lengths):
    chips = lax.axis_size("ctx") // 2
    anywhere = pl.BlockSpec(memory_space=pl.ANY)
    bf16 = jnp.bfloat16
    dma = pltpu.SemaphoreType.DMA
    scratch = [
        pltpu.VMEM((2, 2, PAIR, WIDE), bf16),
        pltpu.VMEM((2, 2, PAIR, WIDE), bf16),
        pltpu.VMEM((2, 2, WINDOW, 2 * HEAD), bf16),
        pltpu.VMEM((2, 2, PAIR, WIDE), bf16),
        pltpu.VMEM((2, 2, PAIR, WIDE), bf16),
        pltpu.VMEM((2, 2, 3 * PAIR, 2 * HEAD), jnp.float32),
        pltpu.VMEM((2, 2, 2 * PAIR, 2 * HEAD), bf16),
        pltpu.VMEM((2, 2, 2 * PAIR, 2 * HEAD), bf16),
        pltpu.VMEM((2, 2, 2 * PAIR, 2 * HEAD), bf16),
        pltpu.VMEM((2, 2, 2, PAIR, 2 * HEAD), bf16),
        pltpu.VMEM((2, 2, PAIR, 2 * HEAD), bf16),
        dma((2, 2, 2, 2)),
        dma((2, 2, 2, 2)),
        dma((2, 2, 2, 2)),
        dma((2, 2, 4)),
        dma((2, 2, 4)),
        dma((2, 2, 3)),
        dma((2, 2, 3)),
    ] + [dma((2, 2, 2)) for _ in range(6)]
    hbm = pl.BlockSpec(memory_space=pltpu.HBM)
    rows = queries.shape[0]
    outs = (queries, queries, key_rows, value_rows)
    packed = pl.pallas_call(
        functools.partial(kernel, chips),
        out_shape=jax.ShapeDtypeStruct((rows, sum(a.shape[1] for a in outs)), bf16),
        in_specs=[pl.BlockSpec(memory_space=pltpu.SMEM)] + [hbm] * 4,
        out_specs=anywhere,
        scratch_shapes=scratch,
        compiler_params=pltpu.CompilerParams(
            collective_id=0, has_side_effects=True, vmem_limit_bytes=61 * 1024 * 1024
        ),
    )(lengths, queries, key_rows, value_rows, output_gradient)
    return pl.pallas_call(
        split_kernel,
        out_shape=tuple(jax.ShapeDtypeStruct(a.shape, bf16) for a in outs),
        in_specs=[anywhere],
        out_specs=(hbm,) * 4,
        scratch_shapes=[pltpu.VMEM(a.shape, bf16) for a in outs] + [dma((2, 4))],
    )(packed)


def solution(mesh):
    rows = P(("groups", "ctx"), None)
    return jax.shard_map(
        on_device,
        mesh=mesh,
        in_specs=(rows, rows, rows, rows, P("groups")),
        out_specs=(rows, rows, rows, rows),
        check_vma=False,
    )
```

```python
import functools
import math

import jax
import jax.numpy as jnp
from jax import lax
from jax.experimental import pallas as pl
from jax.experimental.pallas import tpu as pltpu
from jax.sharding import PartitionSpec as P

KV_HEADS = 4
HEAD = 128
GROUP = 4
HALF_HEADS = KV_HEADS // 2
PAIR = 128
BLOCK = 64
WINDOW = 5 * PAIR
WIDE = GROUP * HEAD
NEGATIVE_FLOOR = -1e30
SCALE = 1.0 / math.sqrt(HEAD)


def kernel(
    chips,
    lengths_ref,
    q_hbm,
    k_hbm,
    v_hbm,
    g_hbm,
    packed,
    qbuf,
    gbuf,
    kvbuf,
    obuf,
    dqbuf,
    kept,
    up_send,
    up_recv,
    sum_send,
    sum_recv,
    final,
    local_sem,
    swap_send,
    swap_recv,
    kv_send,
    kv_recv,
    grad_send,
    grad_recv,
    direct_send,
    out_local,
    out_send,
    out_recv,
    fin_local,
    fin_send,
    fin_recv,
):
    ctx = lax.axis_index("ctx")
    chip = ctx // 2
    core = ctx - 2 * chip
    other = 1 - core
    sibling = 2 * chip + other
    last = 2 * chips - 1

    def place(side):
        return chip + side * (last - 2 * chip)

    def half_of(side, core_id):
        return core_id + side * (1 - 2 * core_id)

    def owner(t):
        return jnp.where(t < chips, t, last - t)

    def side_of(t):
        return jnp.where(t < chips, 0, 1)

    def remote(src, dst, send, recv, device):
        return pltpu.make_async_remote_copy(
            src_ref=src,
            dst_ref=dst,
            send_sem=send,
            recv_sem=recv,
            device_id={"ctx": device},
            device_id_type=pl.DeviceIdType.MESH,
        )

    partner = 2 * (chip + 1 - 2 * lax.rem(chip, 2)) + core

    def odd(s):
        return lax.rem(place(s), 2) == 1

    for slot in range(4):

        @pl.when(chip + slot < 4)
        def _():
            for h in range(HALF_HEADS):
                kvbuf[0, h, slot * PAIR : (slot + 1) * PAIR, :] = jnp.zeros(
                    (PAIR, 2 * HEAD), jnp.bfloat16
                )

    barrier = pltpu.get_barrier_semaphore()

    def greet(device):
        pl.semaphore_signal(
            barrier, inc=1, device_id={"ctx": device}, device_id_type=pl.DeviceIdType.MESH
        )

    count = 3
    greet(sibling)
    for which in range(2):
        greet(partner - core + which)
    for step in (-2, 2):
        peer = chip + step
        near = (peer >= 0) & (peer < chips)

        @pl.when(near)
        def _():
            for which in range(2):
                greet(2 * peer + which)

        count = count + jnp.where(near, 2, 0)
    pl.semaphore_wait(barrier, count)

    def kv_stage(s, h, x, who):
        src = (k_hbm, v_hbm)[x].at[
            pl.ds(s * BLOCK, BLOCK), pl.ds(pl.multiple_of((who * HALF_HEADS + h) * HEAD, HEAD), HEAD)
        ]
        rows = pl.multiple_of(4 * PAIR + half_of(s, core) * BLOCK, BLOCK)
        dst = kvbuf.at[s, h, pl.ds(rows, BLOCK), pl.ds(x * HEAD, HEAD)]
        return src, dst

    def q_stage(s, h, x, who):
        src = (q_hbm, g_hbm)[x].at[
            pl.ds(s * BLOCK, BLOCK), pl.ds(pl.multiple_of((who * HALF_HEADS + h) * WIDE, WIDE), WIDE)
        ]
        rows = pl.multiple_of(half_of(s, core) * BLOCK, BLOCK)
        dst = (qbuf, gbuf)[x].at[s, h, pl.ds(rows, BLOCK), :]
        return src, dst

    def staged_mine(kind, s, h, x):
        src, dst = (kv_stage, q_stage)[kind](s, h, x, core)
        return pltpu.make_async_copy(src, dst, local_sem.at[kind, s, h, x])

    def staged_swap(kind, s, h, x):
        src, dst = (kv_stage, q_stage)[kind](s, h, x, other)
        return remote(
            src, dst, swap_send.at[kind, s, h, x], swap_recv.at[kind, s, h, x], sibling
        )

    def rows_of(slot):
        return pl.ds(slot * PAIR, PAIR)

    def forward(s, h, kind):
        t = place(s) + 2
        source, target = ((4, 3), (4, 2), (2, 0), (3, 1))[kind]
        return remote(
            kvbuf.at[s, h, rows_of(source), :],
            kvbuf.at[side_of(t), h, rows_of(target), :],
            kv_send.at[s, h, kind],
            kv_recv.at[side_of(t), h, kind],
            2 * owner(t) + core,
        )

    def across(s, h, source):
        return remote(
            kvbuf.at[s, h, rows_of(source), :],
            kvbuf.at[s, h, rows_of(3), :],
            kv_send.at[s, h, 0],
            kv_recv.at[s, h, 0],
            partner,
        )

    def arrived(s, h, kind):
        ref = kvbuf.at[s, h, rows_of((3, 2, 0, 1)[kind]), :]
        return remote(ref, ref, kv_send.at[s, h, kind], kv_recv.at[s, h, kind], sibling)

    def sends_own(t):
        return (t + 2 <= last) & (t + 2 != chips)

    def sends_relay(t):
        return sends_own(t) & (t + 2 != chips + 1)

    def odd_across(t):
        return (lax.rem(t, 2) == 1) & (t >= 3) & (t != chips + 1)

    def even_across(t):
        return (lax.rem(t, 2) == 0) & (t >= 2) & (t != chips)

    def direct(s, head, x, kind):
        t = place(s) + 2 * kind
        core_to = head // HALF_HEADS
        h = head % HALF_HEADS
        src = (k_hbm, v_hbm)[x].at[pl.ds(s * BLOCK, BLOCK), pl.ds(head * HEAD, HEAD)]
        rows = pl.multiple_of((3 - kind) * PAIR + half_of(s, core) * BLOCK, BLOCK)
        side = side_of(t) if kind else s
        return remote(
            src,
            kvbuf.at[side, h, pl.ds(rows, BLOCK), pl.ds(x * HEAD, HEAD)],
            direct_send.at[s, head, x, kind],
            kv_recv.at[side, h, kind],
            (2 * owner(t) if kind else partner - core) + core_to,
        )

    def each_direct(s, h, act):
        def run(kind):
            for head in (h, h + HALF_HEADS):
                for x in range(2):
                    act(direct(s, head, x, kind))

        pl.when(sends_own(place(s)))(functools.partial(run, 1))
        pl.when(jnp.logical_not(odd(s)))(functools.partial(run, 0))

    for h in range(HALF_HEADS):
        for s in range(2):
            each_direct(s, h, lambda copy: copy.start())
    order = [(s, h, x) for h in range(HALF_HEADS) for s in range(2) for x in range(2)]
    for kind in range(2):
        for s, h, x in order:
            staged_swap(kind, s, h, x).start()
            staged_mine(kind, s, h, x).start()

    for s, h, x in order:
        staged_mine(0, s, h, x).wait()
        staged_swap(0, s, h, x).wait_recv()

    for h in range(HALF_HEADS):
        for s in range(2):
            here = place(s)
            pl.when((here >= 2) & (here != chips))(arrived(s, h, 1).wait_recv)
            pl.when(odd_across(here))(across(s, h, 2).start)
            pl.when((here >= 2) & (here != chips) & sends_relay(here))(forward(s, h, 2).start)

    for h in range(HALF_HEADS):
        for s in range(2):
            here = place(s)
            pl.when(odd(s) | even_across(here))(arrived(s, h, 0).wait_recv)
            if s == 1:

                @pl.when(here == chips)
                def _():
                    kvbuf[1, h, 2 * PAIR : 4 * PAIR, :] = kvbuf[0, h, 3 * PAIR : 5 * PAIR, :]
                    forward(1, h, 2).start()

            pl.when((here >= 1) & sends_relay(here))(forward(s, h, 3).start)

    def out_place(s, h, x):
        columns = pl.ds(
            pl.multiple_of(x * KV_HEADS * WIDE + (core * HALF_HEADS + h) * WIDE, WIDE), WIDE
        )
        return packed.at[pl.ds(pl.multiple_of(s * BLOCK, BLOCK), BLOCK), columns]

    def fin_place(s, h, x):
        start = 2 * KV_HEADS * WIDE + x * KV_HEADS * HEAD
        columns = pl.ds(pl.multiple_of(start + (core * HALF_HEADS + h) * HEAD, HEAD), HEAD)
        return packed.at[pl.ds(pl.multiple_of(s * BLOCK, BLOCK), BLOCK), columns]

    def half_rows(s, who):
        return pl.ds(pl.multiple_of(half_of(s, who) * BLOCK, BLOCK), BLOCK)

    def out_mine(s, h, x):
        src = (obuf, dqbuf)[x].at[s, h, half_rows(s, core), :]
        return pltpu.make_async_copy(src, out_place(s, h, x), out_local.at[s, h, x])

    def out_swap(s, h, x):
        src = (obuf, dqbuf)[x].at[s, h, half_rows(s, other), :]
        return remote(
            src, out_place(s, h, x), out_send.at[s, h, x], out_recv.at[s, h, x], sibling
        )

    def fin_mine(s, h, x):
        src = final.at[s, h, half_rows(s, core), pl.ds(x * HEAD, HEAD)]
        return pltpu.make_async_copy(src, fin_place(s, h, x), fin_local.at[s, h, x])

    def fin_swap(s, h, x):
        src = final.at[s, h, half_rows(s, other), pl.ds(x * HEAD, HEAD)]
        return remote(
            src, fin_place(s, h, x), fin_send.at[s, h, x], fin_recv.at[s, h, x], sibling
        )

    def partial_up(s, h, slot):
        t = place(s) - 2
        return remote(
            up_send.at[s, h, rows_of(slot), :],
            up_recv.at[side_of(t), h, rows_of(slot), :],
            grad_send.at[s, h, 3 - slot],
            grad_recv.at[side_of(t), h, 3 - slot],
            2 * owner(t) + core,
        )

    def summed_back(s, h):
        t = place(s) - 2
        return remote(
            sum_send.at[s, h, pl.ds(0, PAIR), :],
            sum_recv.at[side_of(t), h, 1],
            grad_send.at[s, h, 1],
            grad_recv.at[side_of(t), h, 1],
            2 * owner(t) + core,
        )

    def summed_across(s, h):
        return remote(
            sum_send.at[s, h, pl.ds(PAIR, PAIR), :],
            sum_recv.at[s, h, 0],
            grad_send.at[s, h, 0],
            grad_recv.at[s, h, 0],
            partner,
        )

    def grad_arrived(s, h, kind):
        if kind >= 2:
            ref = up_recv.at[s, h, rows_of(3 - kind), :]
        else:
            ref = sum_recv.at[s, h, kind]
        return remote(ref, ref, grad_send.at[s, h, kind], grad_recv.at[s, h, kind], sibling)

    def sends_up(t):
        return (t >= 2) & (t != chips) & (t != chips + 1)

    def sends_back(t):
        return (t >= 2) & (t != chips)

    def compute(s, h):
        here = place(s)
        for x in range(2):
            staged_mine(1, s, h, x).wait()
            staged_swap(1, s, h, x).wait_recv()
        relayed = (here != chips) & (here != chips + 1)
        relayed = relayed & jnp.logical_not((s == 0) & (chip == chips - 1))
        pl.when((here >= 4) & relayed)(arrived(s, h, 2).wait_recv)
        pl.when((here >= 3) & relayed)(arrived(s, h, 3).wait_recv)


        query_at = here * PAIR + lax.broadcasted_iota(jnp.int32, (1, PAIR), 1)
        start = jnp.zeros((1, PAIR), jnp.int32)
        end = jnp.int32(0)
        for doc in range(lengths_ref.shape[0]):
            end = end + lengths_ref[doc]
            start = jnp.maximum(start, jnp.where(end <= query_at, end, 0))
        key_at = (here - 4) * PAIR + lax.broadcasted_iota(jnp.int32, (WINDOW, PAIR), 0)
        visible = (key_at >= start) & (key_at <= query_at)
        bias = jnp.where(visible, 0.0, NEGATIVE_FLOOR).astype(jnp.float32)
        bias = jnp.concatenate([bias] * GROUP, axis=1)

        @pl.when(here == chips)
        def _():
            before = place(0)
            pl.when(before >= 4)(arrived(0, h, 2).wait_recv)
            pl.when(before >= 3)(arrived(0, h, 3).wait_recv)
            kvbuf[1, h, 0 : 2 * PAIR, :] = kvbuf[0, h, PAIR : 3 * PAIR, :]

        @pl.when(here == chips + 1)
        def _():
            kvbuf[1, h, 0 : 2 * PAIR, :] = kvbuf[0, h, 3 * PAIR : 5 * PAIR, :]

        keys = kvbuf[s, h, :, 0:HEAD]
        values = kvbuf[s, h, :, HEAD : 2 * HEAD]
        q = jnp.concatenate(
            [qbuf[s, h, :, g * HEAD : (g + 1) * HEAD] for g in range(GROUP)], axis=0
        )
        grad = jnp.concatenate(
            [gbuf[s, h, :, g * HEAD : (g + 1) * HEAD] for g in range(GROUP)], axis=0
        )
        grad_t = grad.T
        scores = lax.dot_general(
            keys, q, (((1,), (1,)), ((), ())), preferred_element_type=jnp.float32
        )
        scores = scores + bias
        top = jnp.max(scores, axis=0, keepdims=True)
        weights = jnp.exp2((scores - top) * (SCALE * math.log2(math.e)))
        total = jnp.sum(weights, axis=0, keepdims=True)
        probs = weights * (1.0 / total)
        probs_b = probs.astype(jnp.bfloat16)
        attended_t = jnp.dot(values.T, probs_b, preferred_element_type=jnp.float32)
        attended_b = attended_t.astype(jnp.bfloat16)
        delta = jnp.sum(
            attended_b.astype(jnp.float32) * grad_t.astype(jnp.float32), axis=0, keepdims=True
        )
        dprob = jnp.dot(values, grad_t, preferred_element_type=jnp.float32)
        dscore = (probs * (dprob - delta)).astype(jnp.bfloat16)
        dq_t = jnp.dot(keys.T, dscore, preferred_element_type=jnp.float32) * SCALE
        dk = jnp.dot(dscore, q, preferred_element_type=jnp.float32) * SCALE
        dv = jnp.dot(probs_b, grad, preferred_element_type=jnp.float32)
        attended = attended_b.T
        dq = dq_t.astype(jnp.bfloat16).T
        for g in range(GROUP):
            obuf[s, h, :, g * HEAD : (g + 1) * HEAD] = attended[g * PAIR : (g + 1) * PAIR]
            dqbuf[s, h, :, g * HEAD : (g + 1) * HEAD] = dq[g * PAIR : (g + 1) * PAIR]
        up_send[s, h, :, 0:HEAD] = dk[0 : 2 * PAIR].astype(jnp.bfloat16)
        up_send[s, h, :, HEAD : 2 * HEAD] = dv[0 : 2 * PAIR].astype(jnp.bfloat16)
        kept[s, h, :, 0:HEAD] = dk[2 * PAIR :]
        kept[s, h, :, HEAD : 2 * HEAD] = dv[2 * PAIR :]

        @pl.when((s == 0) & (chip == chips - 1))
        def _():
            up_send[0, h, PAIR:, :] += up_send[1, h, 0:PAIR, :]
            kept[0, h, 0:PAIR, :] += up_send[1, h, PAIR:, :].astype(jnp.float32)

        @pl.when((s == 0) & (chip == chips - 2))
        def _():
            kept[0, h, PAIR:, :] += up_send[1, h].astype(jnp.float32)

        for slot in (1, 0):
            pl.when(sends_up(here))(partial_up(s, h, slot).start)
        for x in range(2):
            out_swap(s, h, x).start()
            out_mine(s, h, x).start()

    def pass_down(s, h):
        here = place(s)

        def gather(slot):
            first = slot * PAIR

            @pl.when(sends_relay(here))
            def _():
                grad_arrived(s, h, 3 - slot).wait_recv()
                kept[s, h, first : first + PAIR, :] += up_recv[
                    s, h, first : first + PAIR, :
                ].astype(jnp.float32)

            @pl.when(here == chips)
            def _():
                kept[0, h, first + PAIR : first + 2 * PAIR, :] += kept[
                    1, h, first : first + PAIR, :
                ]

        gather(1)
        sum_send[s, h, PAIR:, :] = kept[s, h, PAIR : 2 * PAIR, :].astype(jnp.bfloat16)
        pl.when(odd(s) | even_across(here))(summed_across(s, h).start)
        gather(0)

        @pl.when(jnp.logical_not(odd(s)))
        def _():
            sum_send[s, h, 0:PAIR, :] = kept[s, h, 0:PAIR, :].astype(jnp.bfloat16)
            pl.when(sends_back(here))(summed_back(s, h).start)

    def pass_odd(s, h):
        here = place(s)

        @pl.when(odd(s))
        def _():
            @pl.when(odd_across(here))
            def _():
                grad_arrived(s, h, 0).wait_recv()
                kept[s, h, 0:PAIR, :] += sum_recv[s, h, 0].astype(jnp.float32)

            sum_send[s, h, 0:PAIR, :] = kept[s, h, 0:PAIR, :].astype(jnp.bfloat16)
            pl.when(sends_back(here))(summed_back(s, h).start)

    def finish(s, h):
        here = place(s)

        @pl.when(jnp.logical_not(odd(s)))
        def _():
            grad_arrived(s, h, 0).wait_recv()
            kept[s, h, 2 * PAIR :, :] += sum_recv[s, h, 0].astype(jnp.float32)

        @pl.when(sends_own(here))
        def _():
            grad_arrived(s, h, 1).wait_recv()
            kept[s, h, 2 * PAIR :, :] += sum_recv[s, h, 1].astype(jnp.float32)

        final[s, h] = kept[s, h, 2 * PAIR :, :].astype(jnp.bfloat16)
        for x in range(2):
            fin_swap(s, h, x).start()
            fin_mine(s, h, x).start()

    def turn(i, carry):
        side = 1 - lax.rem(i, 2)
        half = i // 2

        compute(side, half)

        @pl.when(i >= 2)
        def _():
            pass_down(side, half - 1)

        return carry

    lax.fori_loop(0, 4, turn, 0)
    for s in range(2):
        pass_odd(s, 0)
    for s in (1, 0):
        pass_down(s, 1)
    for s in range(2):
        pass_odd(s, 1)
    for h in range(HALF_HEADS):
        for s in range(2):
            finish(s, h)

    for h in range(HALF_HEADS):
        for s in range(2):
            here = place(s)
            for x in range(2):
                for kind in range(2):
                    staged_swap(kind, s, h, x).wait_send()
                out_mine(s, h, x).wait()
                fin_mine(s, h, x).wait()
                for swap in (out_swap, fin_swap):
                    swap(s, h, x).wait_send()
                    swap(s, h, x).wait_recv()
            each_direct(s, h, lambda copy: copy.wait_send())
            pl.when(odd_across(here))(across(s, h, 2).wait_send)
            pl.when((here >= 2) & sends_relay(here))(forward(s, h, 2).wait_send)
            pl.when((here >= 1) & sends_relay(here))(forward(s, h, 3).wait_send)
            for slot in (1, 0):
                pl.when(sends_up(here))(partial_up(s, h, slot).wait_send)
            pl.when(odd(s) | even_across(here))(summed_across(s, h).wait_send)
            pl.when(sends_back(here))(summed_back(s, h).wait_send)


def split_kernel(packed, out, dq, dk, dv, b0, b1, b2, b3, sem):
    ins, outs = [], []
    start = 0
    for i, (ref, buf) in enumerate(zip((out, dq, dk, dv), (b0, b1, b2, b3))):
        width = ref.shape[1]
        ins.append(pltpu.make_async_copy(packed.at[:, pl.ds(start, width)], buf, sem.at[0, i]))
        outs.append(pltpu.make_async_copy(buf, ref, sem.at[1, i]))
        start += width
    for copy in ins:
        copy.start()
    for a, b in zip(ins, outs):
        a.wait()
        b.start()
    for copy in outs:
        copy.wait()


def on_device(queries, key_rows, value_rows, output_gradient, lengths):
    chips = lax.axis_size("ctx") // 2
    anywhere = pl.BlockSpec(memory_space=pl.ANY)
    bf16 = jnp.bfloat16
    dma = pltpu.SemaphoreType.DMA
    scratch = [
        pltpu.VMEM((2, 2, PAIR, WIDE), bf16),
        pltpu.VMEM((2, 2, PAIR, WIDE), bf16),
        pltpu.VMEM((2, 2, WINDOW, 2 * HEAD), bf16),
        pltpu.VMEM((2, 2, PAIR, WIDE), bf16),
        pltpu.VMEM((2, 2, PAIR, WIDE), bf16),
        pltpu.VMEM((2, 2, 3 * PAIR, 2 * HEAD), jnp.float32),
        pltpu.VMEM((2, 2, 2 * PAIR, 2 * HEAD), bf16),
        pltpu.VMEM((2, 2, 2 * PAIR, 2 * HEAD), bf16),
        pltpu.VMEM((2, 2, 2 * PAIR, 2 * HEAD), bf16),
        pltpu.VMEM((2, 2, 2, PAIR, 2 * HEAD), bf16),
        pltpu.VMEM((2, 2, PAIR, 2 * HEAD), bf16),
        dma((2, 2, 2, 2)),
        dma((2, 2, 2, 2)),
        dma((2, 2, 2, 2)),
        dma((2, 2, 4)),
        dma((2, 2, 4)),
        dma((2, 2, 4)),
        dma((2, 2, 4)),
        dma((2, 4, 2, 2)),
    ] + [dma((2, 2, 2)) for _ in range(6)]
    hbm = pl.BlockSpec(memory_space=pltpu.HBM)
    rows = queries.shape[0]
    outs = (queries, queries, key_rows, value_rows)
    packed = pl.pallas_call(
        functools.partial(kernel, chips),
        out_shape=jax.ShapeDtypeStruct((rows, sum(a.shape[1] for a in outs)), bf16),
        in_specs=[pl.BlockSpec(memory_space=pltpu.SMEM)] + [hbm] * 4,
        out_specs=anywhere,
        scratch_shapes=scratch,
        compiler_params=pltpu.CompilerParams(
            collective_id=0, has_side_effects=True, vmem_limit_bytes=61 * 1024 * 1024
        ),
    )(lengths, queries, key_rows, value_rows, output_gradient)
    return pl.pallas_call(
        split_kernel,
        out_shape=tuple(jax.ShapeDtypeStruct(a.shape, bf16) for a in outs),
        in_specs=[anywhere],
        out_specs=(hbm,) * 4,
        scratch_shapes=[pltpu.VMEM(a.shape, bf16) for a in outs] + [dma((2, 4))],
    )(packed)


def solution(mesh):
    rows = P(("groups", "ctx"), None)
    return jax.shard_map(
        on_device,
        mesh=mesh,
        in_specs=(rows, rows, rows, rows, P("groups")),
        out_specs=(rows, rows, rows, rows),
        check_vma=False,
    )
```
